32 devices in a mesh: replica: 4 (over y, x), fsdp: 8 (over z, core).
Axes of the slice: x: 2, y: 2, z: 4, core: 2. Of those that a mesh axis runs over, the one named last changes fastest.
Arguments:
- grad_parts: bfloat16 [4, 4096, 12, 1024], P('replica', 'fsdp'), may hold values from -13 to 13
- col_widths: int32 [12], replicated, may hold values from 512 to 1024, as said below
- assignment: int32 [48], replicated, may hold values from 0 to 7, as said below
- left_stat: float32 [96, 1024, 1024], P('fsdp', 'replica'), may hold values from -1 to 40
- right_stat: float32 [96, 1024, 1024], P('fsdp', 'replica'), may hold values from -1 to 40
- left_root: bfloat16 [96, 1024, 1024], P('fsdp', None, 'replica'), may hold values from -0.25 to 5
- right_root: bfloat16 [96, 1024, 1024], P('fsdp', None, 'replica'), may hold values from -0.25 to 5
Outputs:
- update: bfloat16 [4096, 12, 1024], P('fsdp', None, 'replica')
- left_new: float32 [96, 1024, 1024], P('fsdp', 'replica')
- right_new: float32 [96, 1024, 1024], P('fsdp', 'replica')
The draws below stay inside these ranges and needn't reach their ends.
Inputs may be any that keep to these rules, and one draw needn't show every extreme that they name: `assignment`: each worker index is named by at most 12 blocks, and some worker by exactly 12. `col_widths`: exactly one column block is 512 wide, every other one 1024.
All inputs are finite; a program needn't handle non-finite values.
Results may differ from the reference program's by a relative error of at most 0.012.
Values may be sent and summed in bfloat16 or wider, within the bound.
A program may use at most 256 MiB of HBM per device.

```python
import jax
import jax.numpy as jnp
from jax import lax

D = 4096
BLK = 1024
NCB = 12
NRB = 4
NB = 48
SLOTS = 12
WSLOTS = 96
N_REPLICA = 4
N_FSDP = 8


def diagonal_part(key, lowest, highest, trend):
    position = jnp.arange(BLK, dtype=jnp.float32) / BLK
    spread = jax.random.uniform(key, (WSLOTS, BLK), jnp.float32, jnp.log(lowest), jnp.log(highest))
    return (1.0 + trend * position)[None, :] * jnp.exp(spread)


def assemble(diagonal, offdiag):
    return offdiag + jnp.eye(BLK, dtype=jnp.float32)[None] * diagonal[:, :, None]


def draw_grad_parts(key, part):
    key = jax.random.fold_in(key, 1)
    row_key, col_key, base_key = jax.random.split(key, 3)
    row_pos = (jnp.arange(D) % BLK).astype(jnp.float32) / BLK
    col_pos = jnp.arange(BLK, dtype=jnp.float32) / BLK
    row_scale = jnp.sqrt(1.0 + 2.0 * row_pos) * jnp.exp(jax.random.uniform(row_key, (D,), jnp.float32, -1.15, 1.15))
    col_scale = jnp.sqrt(1.0 + 2.0 * col_pos)[None, :] * jnp.exp(jax.random.uniform(col_key, (NCB, BLK), jnp.float32, -1.15, 1.15))
    base = jnp.clip(jax.random.normal(base_key, (N_REPLICA, D, NCB, BLK), jnp.float32), -5.0, 5.0)
    values = 0.08 * row_scale[None, :, None, None] * col_scale[None, None] * base
    return values.astype(jnp.bfloat16)


def draw_col_widths(key, part):
    key = jax.random.fold_in(key, 2)
    narrow = jax.random.randint(key, (), 0, NCB)
    return jnp.where(jnp.arange(NCB, dtype=jnp.int32) == narrow, BLK // 2, BLK).astype(jnp.int32)


def draw_assignment(key, part):
    key = jax.random.fold_in(key, 3)
    busy_key, block_key, slot_key = jax.random.split(key, 3)
    busiest = jax.random.randint(busy_key, (), 0, N_FSDP)
    shuffled = jax.random.permutation(block_key, NB)
    spare = jax.random.permutation(slot_key, (N_FSDP - 1) * SLOTS)[:NB - SLOTS] // SLOTS
    spare = spare + (spare >= busiest).astype(spare.dtype)
    workers = jnp.concatenate([jnp.full((SLOTS,), busiest, jnp.int32), spare.astype(jnp.int32)])
    return jnp.zeros((NB,), jnp.int32).at[shuffled].set(workers)


def draw_left_stat(key, part):
    key = jax.random.fold_in(key, 4)
    diag_key, off_key = jax.random.split(key)
    diagonal = diagonal_part(diag_key, 1.0, 10.0, 2.0)
    offdiag = 0.1 * jnp.clip(jax.random.normal(off_key, (WSLOTS, BLK, BLK), jnp.float32), -5.0, 5.0)
    return assemble(diagonal, offdiag)


def draw_right_stat(key, part):
    key = jax.random.fold_in(key, 5)
    diag_key, off_key = jax.random.split(key)
    diagonal = diagonal_part(diag_key, 1.0, 10.0, 2.0)
    offdiag = 0.1 * jnp.clip(jax.random.normal(off_key, (WSLOTS, BLK, BLK), jnp.float32), -5.0, 5.0)
    return assemble(diagonal, offdiag)


def draw_left_root(key, part):
    key = jax.random.fold_in(key, 6)
    diag_key, off_key = jax.random.split(key)
    diagonal = diagonal_part(diag_key, 1.0, 2.0, 1.0)
    offdiag = 0.5 / BLK ** 0.5 * jnp.clip(jax.random.normal(off_key, (WSLOTS, BLK, BLK), jnp.float32), -4.0, 4.0)
    return assemble(diagonal, offdiag).astype(jnp.bfloat16)


def draw_right_root(key, part):
    key = jax.random.fold_in(key, 7)
    diag_key, off_key = jax.random.split(key)
    diagonal = diagonal_part(diag_key, 1.0, 2.0, 1.0)
    offdiag = 0.5 / BLK ** 0.5 * jnp.clip(jax.random.normal(off_key, (WSLOTS, BLK, BLK), jnp.float32), -4.0, 4.0)
    return assemble(diagonal, offdiag).astype(jnp.bfloat16)


def setup_inputs(seed: int = 0) -> dict:
    key_of = jax.random.split(jax.random.key(seed), 8)
    return {
        "grad_parts": draw_grad_parts(jax.random.fold_in(key_of[7], 71), 0),
        "col_widths": draw_col_widths(jax.random.fold_in(key_of[7], 71), 0),
        "assignment": draw_assignment(jax.random.fold_in(key_of[7], 71), 0),
        "left_stat": draw_left_stat(jax.random.fold_in(key_of[7], 71), 0),
        "right_stat": draw_right_stat(jax.random.fold_in(key_of[7], 71), 0),
        "left_root": draw_left_root(jax.random.fold_in(key_of[7], 71), 0),
        "right_root": draw_right_root(jax.random.fold_in(key_of[7], 71), 0),
    }


DECAY = 0.99
SHRINKAGE = 0.1
EPSILON = 1e-06

def slot_numbers(assignment):
    blocks = jnp.arange(assignment.shape[0], dtype=jnp.int32)
    same_worker = assignment[:, None] == assignment[None, :]
    earlier = blocks[None, :] < blocks[:, None]
    slot_rank = lax.optimization_barrier(jnp.sum((same_worker & earlier).astype(jnp.int32), axis=1))
    return (assignment * SLOTS + slot_rank).astype(jnp.int32)

def reference(grad_parts, col_widths, assignment, left_stat, right_stat, left_root, right_root):
    col_index = jnp.arange(BLK, dtype=jnp.int32)
    col_mask = (col_index[None, :] < col_widths[:, None]).astype(jnp.float32)
    grad = lax.optimization_barrier(jnp.sum(grad_parts.astype(jnp.float32), axis=0)) * col_mask[None]
    slot_ids = slot_numbers(assignment)
    blocks = jnp.arange(NB, dtype=jnp.int32)

    def one_block(block):
        row_block = (block // NCB).astype(jnp.int32)
        col_block = (block % NCB).astype(jnp.int32)
        slot = slot_ids[block]
        anchor = jnp.zeros((), jnp.int32)
        block_grad = lax.dynamic_slice(grad, (row_block * BLK, col_block, anchor), (BLK, 1, BLK))[:, 0, :]
        width = col_widths[col_block]
        left_gram = jnp.dot(block_grad, block_grad.T, precision=lax.Precision.HIGHEST)
        right_gram = jnp.dot(block_grad.T, block_grad, precision=lax.Precision.HIGHEST)
        left_prod = jnp.dot(left_root[slot], block_grad.astype(jnp.bfloat16), preferred_element_type=jnp.float32).astype(jnp.bfloat16)
        precond = jnp.dot(left_prod, right_root[slot], preferred_element_type=jnp.float32)
        precond = precond * (col_index < width).astype(jnp.float32)[None, :]
        graft = jnp.sqrt(jnp.sum(block_grad * block_grad) / (jnp.sum(precond * precond) + EPSILON))
        return (left_gram, right_gram, (precond * graft).astype(jnp.bfloat16))
    left_grams, right_grams, updates = lax.map(one_block, blocks)
    left_total = (DECAY * left_stat).at[slot_ids].add((1.0 - DECAY) * left_grams)
    right_total = (DECAY * right_stat).at[slot_ids].add((1.0 - DECAY) * right_grams)
    slot_width = jnp.full((WSLOTS,), BLK, jnp.int32).at[slot_ids].set(col_widths[blocks % NCB])
    diag_keep = (col_index[None, :] < slot_width[:, None]).astype(jnp.float32)
    left_trace = jnp.trace(left_total, axis1=1, axis2=2)
    right_trace = lax.optimization_barrier(jnp.sum(jnp.diagonal(right_total, axis1=1, axis2=2) * diag_keep, axis=1))
    unit = jnp.eye(BLK, dtype=jnp.float32)
    left_new = (1.0 - SHRINKAGE) * left_total + SHRINKAGE * (left_trace / BLK)[:, None, None] * unit[None]
    right_scale = SHRINKAGE * right_trace / slot_width.astype(jnp.float32)
    right_new = (1.0 - SHRINKAGE) * right_total + right_scale[:, None, None] * (unit[None] * diag_keep[:, None, :])
    update = updates.reshape(NRB, NCB, BLK, BLK).transpose(0, 2, 1, 3).reshape(D, NCB, BLK)
    return (update, left_new, right_new)
```

```python
import jax
import jax.numpy as jnp
from jax import lax
from jax.experimental import pallas as pl
from jax.experimental.pallas import tpu as pltpu
from jax.sharding import PartitionSpec as P

DECAY = 0.99
SHRINKAGE = 0.1
EPSILON = 1e-06
VMEM = 56 * 1024 * 1024


def slot_tables(assignment, workers, slots):
    blocks = jnp.arange(assignment.shape[0], dtype=jnp.int32)
    same_worker = assignment[:, None] == assignment[None, :]
    earlier = blocks[None, :] < blocks[:, None]
    slot_rank = jnp.sum((same_worker & earlier).astype(jnp.int32), axis=1)
    slot_ids = assignment * slots + slot_rank
    wanted = jnp.arange(workers * slots, dtype=jnp.int32)
    slot_hits = (slot_ids[None, :] == wanted[:, None]).astype(jnp.int32)
    filled = jnp.sum(slot_hits, axis=1) > 0
    block_ids = jnp.sum(slot_hits * blocks[None, :], axis=1)
    return (slot_rank, filled, block_ids)


def pick_body(row, col, live, all_ref, out_ref, sq_ref):
    s = pl.program_id(0)
    per_row, _, rows, quarter = all_ref.shape

    @pl.when(live[s] > 0)
    def _():
        block = all_ref[...].reshape(per_row * rows, quarter)
        out_ref[0] = block
        wide = block.astype(jnp.float32)
        sq_ref[0] = jnp.sum(wide * wide, axis=0, keepdims=True)

    @pl.when(live[s] == 0)
    def _():
        out_ref[...] = jnp.zeros_like(out_ref)
        sq_ref[...] = jnp.zeros_like(sq_ref)


def pick_blocks(shards, row, col, live, per_row):
    workers, ncols, rows, quarter = shards.shape
    slots = row.shape[0]
    return pl.pallas_call(
        pick_body,
        grid_spec=pltpu.PrefetchScalarGridSpec(
            num_scalar_prefetch=3,
            grid=(slots,),
            in_specs=[
                pl.BlockSpec(
                    (per_row, 1, rows, quarter), lambda s, row, col, live: (row[s], col[s], 0, 0)
                )
            ],
            out_specs=[
                pl.BlockSpec((1, per_row * rows, quarter), lambda s, *_: (s, 0, 0)),
                pl.BlockSpec((1, 1, quarter), lambda s, *_: (s, 0, 0)),
            ],
        ),
        out_shape=[
            jax.ShapeDtypeStruct((slots, per_row * rows, quarter), jnp.bfloat16),
            jax.ShapeDtypeStruct((slots, 1, quarter), jnp.float32),
        ],
        compiler_params=pltpu.CompilerParams(vmem_limit_bytes=VMEM),
        name="pick_blocks",
    )(row, col, live, shards)


def step_body(
    ints, lscale, rscale, width, g_ref, l_ref, r_ref, ls_ref, rs_ref,
    ln_ref, rn_ref, pre_ref, sq_ref,
):
    s = pl.program_id(0)
    me, count = ints[0], ints[1]
    n, _, size, quarter = g_ref.shape
    nt = (((1,), (1,)), ((), ()))
    tn = (((0,), (0,)), ((), ()))
    keep = 1.0 - SHRINKAGE
    rows = lax.broadcasted_iota(jnp.int32, (quarter, quarter), 0)
    cols = lax.broadcasted_iota(jnp.int32, (quarter, quarter), 1)
    unit = rows == cols
    first = pl.multiple_of(me * quarter, quarter)

    @pl.when(s < count)
    def _():
        gram = None
        for r in range(n):
            part = lax.dot_general(
                g_ref[r, 0, pl.ds(first, quarter), :], g_ref[r, 0], nt,
                preferred_element_type=jnp.float32,
            )
            gram = part if gram is None else gram + part
        ln_ref[0] = (keep * DECAY) * ls_ref[0] + (keep * (1.0 - DECAY)) * gram
        mine = g_ref[me, 0]
        for r in range(n):
            at = pl.ds(r * quarter, quarter)
            part = lax.dot_general(mine, g_ref[r, 0], tn, preferred_element_type=jnp.float32)
            rn_ref[0, :, at] = (keep * DECAY) * rs_ref[0, :, at] + (keep * (1.0 - DECAY)) * part
        inner = None
        for r in range(n):
            part = jnp.dot(
                g_ref[r, 0], r_ref[0, pl.ds(r * quarter, quarter), :],
                preferred_element_type=jnp.float32,
            )
            inner = part if inner is None else inner + part
        inner = inner.astype(jnp.bfloat16)
        out = None
        for r in range(n):
            part = jnp.dot(
                l_ref[r, 0], inner[r * quarter : (r + 1) * quarter],
                preferred_element_type=jnp.float32,
            )
            out = part if out is None else out + part
        column = lax.broadcasted_iota(jnp.int32, out.shape, 1) + first
        out = jnp.where(column < width[s], out, 0.0)
        sq_ref[0] = jnp.sum(out * out, axis=0, keepdims=True)
        pre_ref[0] = out.astype(jnp.bfloat16)

    @pl.when(s >= count)
    def _():
        ln_ref[0] = (keep * DECAY) * ls_ref[0]
        rn_ref[0] = (keep * DECAY) * rs_ref[0]
        sq_ref[...] = jnp.zeros_like(sq_ref)
        pre_ref[...] = jnp.zeros_like(pre_ref)

    here = pl.ds(first, quarter)
    ln_ref[0, :, here] += jnp.where(unit, lscale[s], 0.0)
    rn_ref[0, :, here] += jnp.where(unit & (rows + first < width[s]), rscale[s], 0.0)


def step_slots(ints, lscale, rscale, width, g_all, l_all, right_root, left_stat, right_stat):
    n, slots, size, quarter = g_all.shape

    def used(s, ints):
        return jnp.minimum(s, jnp.maximum(ints[1] - 1, 0))

    gathered = pl.BlockSpec((n, 1, size, quarter), lambda s, ints, *_: (0, used(s, ints), 0, 0))
    tall = pl.BlockSpec((1, size, quarter), lambda s, ints, *_: (used(s, ints), 0, 0))
    stat = pl.BlockSpec((1, quarter, size), lambda s, *_: (s, 0, 0))
    return pl.pallas_call(
        step_body,
        grid_spec=pltpu.PrefetchScalarGridSpec(
            num_scalar_prefetch=4,
            grid=(slots,),
            in_specs=[gathered, gathered, tall, stat, stat],
            out_specs=[
                stat,
                stat,
                pl.BlockSpec((1, size, quarter), lambda s, *_: (s, 0, 0)),
                pl.BlockSpec((1, 1, quarter), lambda s, *_: (s, 0, 0)),
            ],
        ),
        out_shape=[
            jax.ShapeDtypeStruct(left_stat.shape, jnp.float32),
            jax.ShapeDtypeStruct(right_stat.shape, jnp.float32),
            jax.ShapeDtypeStruct((slots, size, quarter), jnp.bfloat16),
            jax.ShapeDtypeStruct((slots, 1, quarter), jnp.float32),
        ],
        compiler_params=pltpu.CompilerParams(vmem_limit_bytes=VMEM),
        name="step_slots",
    )(ints, lscale, rscale, width, g_all, l_all, right_root, left_stat, right_stat)


def spread_body(slot, mine, scale, pre_ref, out_ref):
    b = pl.program_id(0)
    per_row, _, rows, quarter = out_ref.shape

    @pl.when(mine[b] > 0)
    def _():
        block = pre_ref[0].astype(jnp.float32) * scale[slot[b]]
        out_ref[...] = block.astype(jnp.bfloat16).reshape(out_ref.shape)

    @pl.when(mine[b] == 0)
    def _():
        out_ref[...] = jnp.zeros_like(out_ref)


def spread_blocks(precond, slot, mine, scale, workers, ncols, rows):
    slots, size, quarter = precond.shape
    per_row = size // rows
    return pl.pallas_call(
        spread_body,
        grid_spec=pltpu.PrefetchScalarGridSpec(
            num_scalar_prefetch=3,
            grid=(slot.shape[0],),
            in_specs=[pl.BlockSpec((1, size, quarter), lambda b, slot, *_: (slot[b], 0, 0))],
            out_specs=pl.BlockSpec(
                (per_row, 1, rows, quarter), lambda b, *_: (b // ncols, b % ncols, 0, 0)
            ),
        ),
        out_shape=jax.ShapeDtypeStruct((workers, ncols, rows, quarter), jnp.bfloat16),
        compiler_params=pltpu.CompilerParams(vmem_limit_bytes=VMEM),
        name="spread_blocks",
    )(slot, mine, scale, precond)


def on_device(grad_parts, col_widths, assignment, left_stat, right_stat, left_root, right_root):
    workers = lax.axis_size("fsdp")
    me_rep = lax.axis_index("replica")
    me_work = lax.axis_index("fsdp")
    slots, quarter, block_size = left_stat.shape
    rows_dev, ncols = grad_parts.shape[1:3]
    per_row = block_size // rows_dev
    slot_rank, filled, block_ids = slot_tables(assignment, workers, slots)

    summed = lax.psum_scatter(grad_parts[0], "replica", scatter_dimension=2, tiled=True)
    left_wide = lax.all_gather(left_root, "replica", axis=0)

    my_blocks = lax.dynamic_slice_in_dim(block_ids, me_work * slots, slots)
    my_filled = lax.dynamic_slice_in_dim(filled, me_work * slots, slots)
    my_count = jnp.sum(my_filled.astype(jnp.int32))
    my_row = my_blocks // ncols
    my_col = my_blocks % ncols
    looked_up = jnp.sum(
        jnp.where(
            my_col[:, None] == jnp.arange(ncols, dtype=jnp.int32)[None, :], col_widths[None, :], 0
        ),
        axis=1,
    )
    my_width = jnp.where(my_filled, looked_up, block_size)

    first = me_rep * quarter
    global_rows = first + jnp.arange(quarter, dtype=jnp.int32)
    unit = jnp.eye(quarter, dtype=jnp.float32)
    within = (global_rows[None, :] < my_width[:, None]).astype(jnp.float32)
    left_diag = jnp.sum(lax.dynamic_slice_in_dim(left_stat, first, quarter, 2) * unit, axis=2)
    right_diag = jnp.sum(lax.dynamic_slice_in_dim(right_stat, first, quarter, 2) * unit, axis=2)
    left_part = jnp.sum(left_diag, axis=1)
    right_part = jnp.sum(right_diag * within, axis=1)

    col_mask = global_rows[None, :] < col_widths[:, None]
    masked = jnp.where(col_mask[None], summed, jnp.zeros((), jnp.bfloat16))
    shards = lax.all_gather(jnp.transpose(masked, (1, 0, 2)), "fsdp", axis=0)
    g_cols, g_sq = pick_blocks(shards, my_row, my_col, my_filled.astype(jnp.int32), per_row)
    g_all = lax.all_gather(g_cols, "replica", axis=0)
    left_trace, right_trace, grad_square = lax.psum(
        (left_part, right_part, jnp.sum(g_sq, axis=(1, 2))), "replica"
    )
    left_scale = SHRINKAGE * (DECAY * left_trace + (1.0 - DECAY) * grad_square) / block_size
    right_scale = (
        SHRINKAGE
        * (DECAY * right_trace + (1.0 - DECAY) * grad_square)
        / my_width.astype(jnp.float32)
    )
    ints = jnp.stack([me_rep.astype(jnp.int32), my_count])
    left_new, right_new, precond, p_sq = step_slots(
        ints, left_scale, right_scale, my_width, g_all, left_wide, right_root, left_stat, right_stat
    )
    precond_square = lax.psum(jnp.sum(p_sq, axis=(1, 2)), "replica")
    graft_scale = jnp.sqrt(grad_square / (precond_square + EPSILON))

    mine = (assignment == me_work).astype(jnp.int32)
    outgoing = spread_blocks(
        precond, jnp.where(mine > 0, slot_rank, 0), mine, graft_scale, workers, ncols, rows_dev
    )
    arrived = lax.psum_scatter(outgoing, "fsdp", scatter_dimension=0, tiled=False)
    update = jnp.transpose(arrived, (1, 0, 2))
    return (update, left_new, right_new)


def solution(mesh):
    in_specs = (
        P("replica", "fsdp", None, None),
        P(),
        P(),
        P("fsdp", "replica", None),
        P("fsdp", "replica", None),
        P("fsdp", None, "replica"),
        P("fsdp", None, "replica"),
    )
    out_specs = (P("fsdp", None, "replica"), P("fsdp", "replica", None), P("fsdp", "replica", None))
    return jax.shard_map(
        on_device, mesh=mesh, in_specs=in_specs, out_specs=out_specs, check_vma=False
    )
```

```python
import functools

import jax
import jax.numpy as jnp
from jax import lax
from jax.experimental import pallas as pl
from jax.experimental.pallas import tpu as pltpu
from jax.sharding import PartitionSpec as P

DECAY = 0.99
SHRINKAGE = 0.1
EPSILON = 1e-06
DEPTHS = (4, 5, 6, 7, 8)
VMEM = 56 * 1024 * 1024


def slot_tables(assignment, workers, slots):
    blocks = jnp.arange(assignment.shape[0], dtype=jnp.int32)
    same_worker = assignment[:, None] == assignment[None, :]
    earlier = blocks[None, :] < blocks[:, None]
    slot_rank = jnp.sum((same_worker & earlier).astype(jnp.int32), axis=1)
    slot_ids = assignment * slots + slot_rank
    wanted = jnp.arange(workers * slots, dtype=jnp.int32)
    slot_hits = (slot_ids[None, :] == wanted[:, None]).astype(jnp.int32)
    filled = jnp.sum(slot_hits, axis=1) > 0
    block_ids = jnp.sum(slot_hits * blocks[None, :], axis=1)
    return (slot_rank, filled, block_ids)


def pick_body(row, rank, live, got_ref, out_ref, sq_ref):
    s = pl.program_id(0)
    cores, chips, _, rows, quarter = got_ref.shape

    @pl.when(live[s] > 0)
    def _():
        total = jnp.zeros((1, quarter), jnp.float32)
        for t in range(chips):
            for c in range(cores):
                part = got_ref[c, t, 0]
                out_ref[0, pl.ds((t * cores + c) * rows, rows), :] = part
                wide = part.astype(jnp.float32)
                total = total + jnp.sum(wide * wide, axis=0, keepdims=True)
        sq_ref[0] = total

    @pl.when(live[s] == 0)
    def _():
        out_ref[...] = jnp.zeros_like(out_ref)
        sq_ref[...] = jnp.zeros_like(sq_ref)


def pick_blocks(got, row, rank, live, size):
    cores, _, _, rows, quarter = got.shape
    slots = row.shape[0]
    chips = size // (rows * cores)
    return pl.pallas_call(
        pick_body,
        grid_spec=pltpu.PrefetchScalarGridSpec(
            num_scalar_prefetch=3,
            grid=(slots,),
            in_specs=[
                pl.BlockSpec(
                    (cores, chips, 1, rows, quarter),
                    lambda s, row, rank, live: (0, row[s], rank[s], 0, 0),
                )
            ],
            out_specs=[
                pl.BlockSpec((1, size, quarter), lambda s, *_: (s, 0, 0)),
                pl.BlockSpec((1, 1, quarter), lambda s, *_: (s, 0, 0)),
            ],
        ),
        out_shape=[
            jax.ShapeDtypeStruct((slots, size, quarter), jnp.bfloat16),
            jax.ShapeDtypeStruct((slots, 1, quarter), jnp.float32),
        ],
        compiler_params=pltpu.CompilerParams(vmem_limit_bytes=VMEM),
        name="pick_blocks",
    )(row, rank, live, got)


def fill_body(col, in_ref, out_ref):
    out_ref[0] = in_ref[...]


def fill_outgoing(by_block, col, chips, depth):
    ncols, rows, quarter = by_block.shape
    return pl.pallas_call(
        fill_body,
        grid_spec=pltpu.PrefetchScalarGridSpec(
            num_scalar_prefetch=1,
            grid=(chips, depth),
            in_specs=[pl.BlockSpec((1, rows, quarter), lambda p, k, col: (col[p, k], 0, 0))],
            out_specs=pl.BlockSpec((1, 1, rows, quarter), lambda p, k, *_: (p, k, 0, 0)),
        ),
        out_shape=jax.ShapeDtypeStruct((chips, depth, rows, quarter), jnp.bfloat16),
        compiler_params=pltpu.CompilerParams(vmem_limit_bytes=VMEM),
        name="fill_outgoing",
    )(col, by_block)


def exchange_body(
    chips, depth, share, src, dst, own_sem, send_sem, recv_sem, pass_send, pass_recv
):
    rep = lax.axis_index("replica")
    work = lax.axis_index("fsdp")
    chip = work // 2
    core = work % 2
    sibling = (rep, chip * 2 + 1 - core)
    part = pl.ds(0, depth)

    def landing(p):
        return dst.at[core, p, part] if share else dst.at[p, part]

    def peer(d):
        return lax.rem(chip + d, chips)

    barrier = pltpu.get_barrier_semaphore()
    for d in range(1, chips):
        pl.semaphore_signal(
            barrier, inc=1, device_id=(rep, peer(d) * 2 + core),
            device_id_type=pl.DeviceIdType.MESH,
        )
    if share:
        pl.semaphore_signal(
            barrier, inc=1, device_id=sibling, device_id_type=pl.DeviceIdType.MESH
        )
    pl.semaphore_wait(barrier, chips if share else chips - 1)

    sends = []
    for d in range(1, chips):
        copy = pltpu.make_async_remote_copy(
            src_ref=src.at[peer(d), part],
            dst_ref=landing(chip),
            send_sem=send_sem.at[d],
            recv_sem=recv_sem.at[d],
            device_id=(rep, peer(d) * 2 + core),
            device_id_type=pl.DeviceIdType.MESH,
        )
        copy.start()
        sends.append(copy)
    keep = pltpu.make_async_copy(src.at[chip, part], landing(chip), own_sem)
    keep.start()
    passes = []
    if share:
        copy = pltpu.make_async_remote_copy(
            src_ref=src.at[chip, part],
            dst_ref=landing(chip),
            send_sem=pass_send.at[0],
            recv_sem=pass_recv.at[0],
            device_id=sibling,
            device_id_type=pl.DeviceIdType.MESH,
        )
        copy.start()
        passes.append(copy)
    for d in range(1, chips):
        sends[d - 1].wait_recv()
        if share:
            origin = lax.rem(chip + chips - d, chips)
            copy = pltpu.make_async_remote_copy(
                src_ref=landing(origin),
                dst_ref=landing(origin),
                send_sem=pass_send.at[d],
                recv_sem=pass_recv.at[d],
                device_id=sibling,
                device_id_type=pl.DeviceIdType.MESH,
            )
            copy.start()
            passes.append(copy)
    keep.wait()
    for copy in sends:
        copy.wait_send()
    for copy in passes:
        copy.wait()


def exchange(outgoing, most, share, name_id):
    chips, depth, rows, quarter = outgoing.shape
    shape = (chips, most, rows, quarter)
    if share:
        shape = (2,) + shape
    return pl.pallas_call(
        functools.partial(exchange_body, chips, depth, share),
        out_shape=jax.ShapeDtypeStruct(shape, jnp.bfloat16),
        in_specs=[pl.BlockSpec(memory_space=pl.ANY)],
        out_specs=pl.BlockSpec(memory_space=pl.ANY),
        scratch_shapes=[
            pltpu.SemaphoreType.DMA,
            pltpu.SemaphoreType.DMA((chips,)),
            pltpu.SemaphoreType.DMA((chips,)),
            pltpu.SemaphoreType.DMA((chips,)),
            pltpu.SemaphoreType.DMA((chips,)),
        ],
        compiler_params=pltpu.CompilerParams(
            collective_id=name_id, has_side_effects=True, vmem_limit_bytes=VMEM
        ),
        cost_estimate=pl.CostEstimate(
            flops=0, bytes_accessed=64 * outgoing.size, transcendentals=0
        ),
        name="exchange_in" if share else "exchange_back",
    )(outgoing)


def step_body(
    ints, lscale, rscale, width, g_ref, l_ref, r_ref, ls_ref, rs_ref,
    ln_ref, rn_ref, pre_ref, sq_ref,
):
    s = pl.program_id(0)
    me, count = ints[0], ints[1]
    n, _, size, quarter = g_ref.shape
    nt = (((1,), (1,)), ((), ()))
    tn = (((0,), (0,)), ((), ()))
    keep = 1.0 - SHRINKAGE
    rows = lax.broadcasted_iota(jnp.int32, (quarter, quarter), 0)
    cols = lax.broadcasted_iota(jnp.int32, (quarter, quarter), 1)
    unit = rows == cols
    first = pl.multiple_of(me * quarter, quarter)

    @pl.when(s < count)
    def _():
        gram = None
        for r in range(n):
            part = lax.dot_general(
                g_ref[r, 0, pl.ds(first, quarter), :], g_ref[r, 0], nt,
                preferred_element_type=jnp.float32,
            )
            gram = part if gram is None else gram + part
        ln_ref[0] = (keep * DECAY) * ls_ref[0] + (keep * (1.0 - DECAY)) * gram
        mine = g_ref[me, 0]
        for r in range(n):
            at = pl.ds(r * quarter, quarter)
            part = lax.dot_general(mine, g_ref[r, 0], tn, preferred_element_type=jnp.float32)
            rn_ref[0, :, at] = (keep * DECAY) * rs_ref[0, :, at] + (keep * (1.0 - DECAY)) * part
        inner = None
        for r in range(n):
            part = jnp.dot(
                g_ref[r, 0], r_ref[0, pl.ds(r * quarter, quarter), :],
                preferred_element_type=jnp.float32,
            )
            inner = part if inner is None else inner + part
        inner = inner.astype(jnp.bfloat16)
        out = None
        for r in range(n):
            part = jnp.dot(
                l_ref[r, 0], inner[r * quarter : (r + 1) * quarter],
                preferred_element_type=jnp.float32,
            )
            out = part if out is None else out + part
        column = lax.broadcasted_iota(jnp.int32, out.shape, 1) + first
        out = jnp.where(column < width[s], out, 0.0)
        sq_ref[0] = jnp.sum(out * out, axis=0, keepdims=True)
        pre_ref[0] = out.astype(jnp.bfloat16)

    @pl.when(s >= count)
    def _():
        ln_ref[0] = (keep * DECAY) * ls_ref[0]
        rn_ref[0] = (keep * DECAY) * rs_ref[0]
        sq_ref[...] = jnp.zeros_like(sq_ref)
        pre_ref[...] = jnp.zeros_like(pre_ref)

    here = pl.ds(first, quarter)
    ln_ref[0, :, here] += jnp.where(unit, lscale[s], 0.0)
    rn_ref[0, :, here] += jnp.where(unit & (rows + first < width[s]), rscale[s], 0.0)


def step_slots(ints, lscale, rscale, width, g_all, l_all, right_root, left_stat, right_stat):
    n, slots, size, quarter = g_all.shape

    def used(s, ints):
        return jnp.minimum(s, jnp.maximum(ints[1] - 1, 0))

    gathered = pl.BlockSpec((n, 1, size, quarter), lambda s, ints, *_: (0, used(s, ints), 0, 0))
    tall = pl.BlockSpec((1, size, quarter), lambda s, ints, *_: (used(s, ints), 0, 0))
    stat = pl.BlockSpec((1, quarter, size), lambda s, *_: (s, 0, 0))
    return pl.pallas_call(
        step_body,
        grid_spec=pltpu.PrefetchScalarGridSpec(
            num_scalar_prefetch=4,
            grid=(slots,),
            in_specs=[gathered, gathered, tall, stat, stat],
            out_specs=[
                stat,
                stat,
                pl.BlockSpec((1, size, quarter), lambda s, *_: (s, 0, 0)),
                pl.BlockSpec((1, 1, quarter), lambda s, *_: (s, 0, 0)),
            ],
        ),
        out_shape=[
            jax.ShapeDtypeStruct(left_stat.shape, jnp.float32),
            jax.ShapeDtypeStruct(right_stat.shape, jnp.float32),
            jax.ShapeDtypeStruct((slots, size, quarter), jnp.bfloat16),
            jax.ShapeDtypeStruct((slots, 1, quarter), jnp.float32),
        ],
        compiler_params=pltpu.CompilerParams(vmem_limit_bytes=VMEM),
        name="step_slots",
    )(ints, lscale, rscale, width, g_all, l_all, right_root, left_stat, right_stat)


def load_body(slot, own, core, own_ref, sib_ref, out_ref):
    p, k = pl.program_id(0), pl.program_id(1)

    @pl.when(own[p, k] > 0)
    def _():
        out_ref[0, 0] = own_ref[0, 0, 0]

    @pl.when(own[p, k] == 0)
    def _():
        out_ref[0, 0] = sib_ref[0, 0]


def load_outgoing(mine, sibling, slot, own, core, chips, depth):
    _, hosts, _, rows, quarter = mine.shape
    return pl.pallas_call(
        load_body,
        grid_spec=pltpu.PrefetchScalarGridSpec(
            num_scalar_prefetch=3,
            grid=(chips, depth),
            in_specs=[
                pl.BlockSpec(
                    (1, 1, 1, rows, quarter),
                    lambda p, k, slot, own, core: (slot[p, k], p % hosts, core[0], 0, 0),
                ),
                pl.BlockSpec(
                    (1, 1, rows, quarter),
                    lambda p, k, slot, own, core: (slot[p, k], p % hosts, 0, 0),
                ),
            ],
            out_specs=pl.BlockSpec((1, 1, rows, quarter), lambda p, k, *_: (p, k, 0, 0)),
        ),
        out_shape=jax.ShapeDtypeStruct((chips, depth, rows, quarter), jnp.bfloat16),
        compiler_params=pltpu.CompilerParams(vmem_limit_bytes=VMEM),
        name="load_outgoing",
    )(slot, own, core, mine, sibling)


def assemble_body(chip, rank, scale, in_ref, out_ref):
    j = pl.program_id(0)
    out_ref[0] = (in_ref[0, 0].astype(jnp.float32) * scale[j]).astype(jnp.bfloat16)


def assemble(got, chip, rank, scale):
    _, _, rows, quarter = got.shape
    return pl.pallas_call(
        assemble_body,
        grid_spec=pltpu.PrefetchScalarGridSpec(
            num_scalar_prefetch=3,
            grid=(chip.shape[0],),
            in_specs=[
                pl.BlockSpec(
                    (1, 1, rows, quarter), lambda j, chip, rank, scale: (chip[j], rank[j], 0, 0)
                )
            ],
            out_specs=pl.BlockSpec((1, rows, quarter), lambda j, *_: (j, 0, 0)),
        ),
        out_shape=jax.ShapeDtypeStruct((chip.shape[0], rows, quarter), jnp.bfloat16),
        compiler_params=pltpu.CompilerParams(vmem_limit_bytes=VMEM),
        name="assemble",
    )(chip, rank, scale, got)


def on_device(grad_parts, col_widths, assignment, left_stat, right_stat, left_root, right_root):
    workers = lax.axis_size("fsdp")
    me_rep = lax.axis_index("replica")
    me_work = lax.axis_index("fsdp")
    slots, quarter, block_size = left_stat.shape
    rows_dev, ncols = grad_parts.shape[1:3]
    per_row = block_size // rows_dev
    chips = workers // 2
    hosts = per_row // 2
    chip, core = me_work // 2, me_work % 2
    most = min(ncols, 2 * slots)
    cases = [k for k in DEPTHS if k < most] + [most]
    slot_rank, filled, block_ids = slot_tables(assignment, workers, slots)
    blocks = jnp.arange(assignment.shape[0], dtype=jnp.int32)
    of_row = blocks // ncols
    of_chip = assignment // 2
    pair = of_row * chips + of_chip
    pair_rank = jnp.sum(
        ((pair[:, None] == pair[None, :]) & (blocks[None, :] < blocks[:, None])).astype(jnp.int32),
        axis=1,
    )
    depth = jnp.max(pair_rank) + 1
    case = sum((depth > k).astype(jnp.int32) for k in cases[:-1]) if len(cases) > 1 else None
    owner_first = me_work // per_row * ncols
    row_chip = lax.dynamic_slice_in_dim(of_chip, owner_first, ncols)
    row_rank = lax.dynamic_slice_in_dim(pair_rank, owner_first, ncols)
    all_chips = jnp.arange(chips, dtype=jnp.int32)
    ranks = jnp.arange(most, dtype=jnp.int32)
    leaves = (row_chip == all_chips[:, None, None]) & (row_rank == ranks[None, :, None])
    send_col = jnp.sum(jnp.where(leaves, jnp.arange(ncols, dtype=jnp.int32), 0), axis=2)
    returns = (
        (of_chip == chip)
        & (of_row == (all_chips // hosts)[:, None, None])
        & (pair_rank == ranks[None, :, None])
    )
    back_slot = jnp.sum(jnp.where(returns, slot_rank, 0), axis=2)
    back_own = jnp.sum((returns & (assignment == me_work)).astype(jnp.int32), axis=2)

    def by_depth(make, *args):
        if len(cases) == 1:
            return make(0, *args)
        return lax.switch(case, [functools.partial(make, n) for n in range(len(cases))], *args)

    summed = lax.psum_scatter(grad_parts[0], "replica", scatter_dimension=2, tiled=True)
    left_wide = lax.all_gather(left_root, "replica", axis=0)

    my_blocks = lax.dynamic_slice_in_dim(block_ids, me_work * slots, slots)
    my_filled = lax.dynamic_slice_in_dim(filled, me_work * slots, slots)
    my_count = jnp.sum(my_filled.astype(jnp.int32))
    my_row = my_blocks // ncols
    my_col = my_blocks % ncols
    looked_up = jnp.sum(
        jnp.where(
            my_col[:, None] == jnp.arange(ncols, dtype=jnp.int32)[None, :], col_widths[None, :], 0
        ),
        axis=1,
    )
    my_width = jnp.where(my_filled, looked_up, block_size)

    first = me_rep * quarter
    global_rows = first + jnp.arange(quarter, dtype=jnp.int32)
    unit = jnp.eye(quarter, dtype=jnp.float32)
    within = (global_rows[None, :] < my_width[:, None]).astype(jnp.float32)
    left_diag = jnp.sum(lax.dynamic_slice_in_dim(left_stat, first, quarter, 2) * unit, axis=2)
    right_diag = jnp.sum(lax.dynamic_slice_in_dim(right_stat, first, quarter, 2) * unit, axis=2)
    left_part = jnp.sum(left_diag, axis=1)
    right_part = jnp.sum(right_diag * within, axis=1)

    col_mask = global_rows[None, :] < col_widths[:, None]
    masked = jnp.where(col_mask[None], summed, jnp.zeros((), jnp.bfloat16))

    def send_in(n, by_block, col):
        outgoing = fill_outgoing(by_block, col, chips, cases[n])
        return exchange(outgoing, most, True, 2 * n)

    got = by_depth(send_in, jnp.transpose(masked, (1, 0, 2)), send_col)
    my_rank = jnp.take(pair_rank, my_blocks)
    g_cols, g_sq = pick_blocks(got, my_row, my_rank, my_filled.astype(jnp.int32), block_size)
    g_all = lax.all_gather(g_cols, "replica", axis=0)
    left_trace, right_trace, grad_square = lax.psum(
        (left_part, right_part, jnp.sum(g_sq, axis=(1, 2))), "replica"
    )
    left_scale = SHRINKAGE * (DECAY * left_trace + (1.0 - DECAY) * grad_square) / block_size
    right_scale = (
        SHRINKAGE
        * (DECAY * right_trace + (1.0 - DECAY) * grad_square)
        / my_width.astype(jnp.float32)
    )
    ints = jnp.stack([me_rep.astype(jnp.int32), my_count])
    left_new, right_new, precond, p_sq = step_slots(
        ints, left_scale, right_scale, my_width, g_all, left_wide, right_root, left_stat, right_stat
    )
    split = precond.reshape(slots, hosts, 2, rows_dev, quarter)
    swap = [(w, w + 1 - 2 * (w % 2)) for w in range(workers)]
    crossing = lax.dynamic_index_in_dim(split, 1 - core, 2, keepdims=False)
    sibling = lax.ppermute(crossing, "fsdp", swap)

    def send_back(n, mine, other, slot, own, core):
        outgoing = load_outgoing(mine, other, slot, own, core, chips, cases[n])
        return exchange(outgoing, most, False, 2 * n + 1)

    back = by_depth(send_back, split, sibling, back_slot, back_own, core[None])
    precond_square = lax.psum(jnp.sum(p_sq, axis=(1, 2)), "replica")
    graft_scale = jnp.sqrt(grad_square / (precond_square + EPSILON))
    every_scale = lax.all_gather(graft_scale, "fsdp", axis=0, tiled=True)
    owner_worker = lax.dynamic_slice_in_dim(assignment, owner_first, ncols)
    owner_slot = lax.dynamic_slice_in_dim(slot_rank, owner_first, ncols)
    my_scale = jnp.take(every_scale, owner_worker * slots + owner_slot)
    arrived = assemble(back, row_chip, row_rank, my_scale)
    update = jnp.transpose(arrived, (1, 0, 2))
    return (update, left_new, right_new)


def solution(mesh):
    in_specs = (
        P("replica", "fsdp", None, None),
        P(),
        P(),
        P("fsdp", "replica", None),
        P("fsdp", "replica", None),
        P("fsdp", None, "replica"),
        P("fsdp", None, "replica"),
    )
    out_specs = (P("fsdp", None, "replica"), P("fsdp", "replica", None), P("fsdp", "replica", None))
    return jax.shard_map(
        on_device, mesh=mesh, in_specs=in_specs, out_specs=out_specs, check_vma=False
    )
```

```python
import functools

import jax
import jax.numpy as jnp
from jax import lax
from jax.experimental import pallas as pl
from jax.experimental.pallas import tpu as pltpu
from jax.sharding import PartitionSpec as P

DECAY = 0.99
SHRINKAGE = 0.1
EPSILON = 1e-06
DEPTHS = (4, 5, 6, 8)
WIDTHS = (8, 9, 10)
REPLICAS = 4
VMEM = 56 * 1024 * 1024


def slot_tables(assignment, workers, slots):
    blocks = jnp.arange(assignment.shape[0], dtype=jnp.int32)
    same_worker = assignment[:, None] == assignment[None, :]
    earlier = blocks[None, :] < blocks[:, None]
    slot_rank = jnp.sum((same_worker & earlier).astype(jnp.int32), axis=1)
    slot_ids = assignment * slots + slot_rank
    wanted = jnp.arange(workers * slots, dtype=jnp.int32)
    slot_hits = (slot_ids[None, :] == wanted[:, None]).astype(jnp.int32)
    filled = jnp.sum(slot_hits, axis=1) > 0
    block_ids = jnp.sum(slot_hits * blocks[None, :], axis=1)
    return (slot_rank, filled, block_ids)


def pick_body(row, rank, live, own_row, own_rank, own_live, got_ref, own_ref, out_ref, sq_ref):
    s = pl.program_id(0)
    cores, chips, _, rows, quarter = got_ref.shape

    @pl.when(live[s] > 0)
    def _():
        for t in range(chips):
            for c in range(cores):
                out_ref[0, pl.ds((t * cores + c) * rows, rows), :] = got_ref[c, t, 0]

    @pl.when(live[s] == 0)
    def _():
        out_ref[...] = jnp.zeros_like(out_ref)

    @pl.when(own_live[s] > 0)
    def _():
        total = jnp.zeros((1, quarter), jnp.float32)
        for t in range(chips):
            for c in range(cores):
                wide = own_ref[c, t, 0].astype(jnp.float32)
                total = total + jnp.sum(wide * wide, axis=0, keepdims=True)
        sq_ref[0] = total

    @pl.when(own_live[s] == 0)
    def _():
        sq_ref[...] = jnp.zeros_like(sq_ref)


def pick_blocks(got, wire, own, size):
    cores, _, _, rows, quarter = got.shape
    slots = own[0].shape[0]
    chips = size // (rows * cores)
    block = (cores, chips, 1, rows, quarter)
    return pl.pallas_call(
        pick_body,
        grid_spec=pltpu.PrefetchScalarGridSpec(
            num_scalar_prefetch=6,
            grid=(slots,),
            in_specs=[
                pl.BlockSpec(block, lambda s, row, rank, *_: (0, row[s], rank[s], 0, 0)),
                pl.BlockSpec(
                    block, lambda s, a, b, c, row, rank, live: (0, row[s], rank[s], 0, 0)
                ),
            ],
            out_specs=[
                pl.BlockSpec((1, size, quarter), lambda s, *_: (s, 0, 0)),
                pl.BlockSpec((1, 1, quarter), lambda s, *_: (s, 0, 0)),
            ],
        ),
        out_shape=[
            jax.ShapeDtypeStruct((slots, size, quarter), jnp.bfloat16),
            jax.ShapeDtypeStruct((slots, 1, quarter), jnp.float32),
        ],
        compiler_params=pltpu.CompilerParams(vmem_limit_bytes=VMEM),
        name="pick_blocks",
    )(*wire, *own, got, got)


def fill_body(col, in_ref, out_ref):
    out_ref[0] = in_ref[...]


def fill_outgoing(by_block, col, chips, depth):
    ncols, rows, quarter = by_block.shape
    return pl.pallas_call(
        fill_body,
        grid_spec=pltpu.PrefetchScalarGridSpec(
            num_scalar_prefetch=1,
            grid=(chips, depth),
            in_specs=[pl.BlockSpec((1, rows, quarter), lambda p, k, col: (col[p, k], 0, 0))],
            out_specs=pl.BlockSpec((1, 1, rows, quarter), lambda p, k, *_: (p, k, 0, 0)),
        ),
        out_shape=jax.ShapeDtypeStruct((chips, depth, rows, quarter), jnp.bfloat16),
        compiler_params=pltpu.CompilerParams(vmem_limit_bytes=VMEM),
        name="fill_outgoing",
    )(col, by_block)


def remote(src, dst, sems, at, device):
    return pltpu.make_async_remote_copy(
        src_ref=src,
        dst_ref=dst,
        send_sem=sems[0].at[at],
        recv_sem=sems[1].at[at],
        device_id=device,
        device_id_type=pl.DeviceIdType.MESH,
    )


def greet(devices):
    barrier = pltpu.get_barrier_semaphore()
    for device in devices:
        pl.semaphore_signal(
            barrier, inc=1, device_id=device, device_id_type=pl.DeviceIdType.MESH
        )
    pl.semaphore_wait(barrier, len(devices))


class Gather:
    def __init__(self, wide, src, dst, own_sem, sems, tail_sems):
        rep, work = lax.axis_index("replica"), lax.axis_index("fsdp")
        self.wide, self.src, self.dst = wide, src, dst
        self.own_sem, self.sems, self.tail_sems = own_sem, sems, tail_sems
        self.rep = rep
        across = rep // 2
        along = rep % 2
        self.x_rep = across * 2 + 1 - along
        self.y_rep = (1 - across) * 2 + along
        self.d_rep = (1 - across) * 2 + 1 - along
        self.x = (self.x_rep, work)
        self.y = (self.y_rep, work)
        self.sibling = (rep, work // 2 * 2 + 1 - work % 2)
        self.slots, self.size = src.shape[:2]

    def devices(self):
        return [self.x, self.y] + ([self.sibling] if self.wide < self.slots else [])

    def half(self, ref, h):
        mid = self.size // 2
        return ref.at[pl.ds(0, self.wide), pl.ds(h * mid, mid)]

    def start(self):
        mine = self.dst.at[self.rep]
        self.out = []
        for at, (to, h) in enumerate([(self.x, 0), (self.y, 1), (self.x, 1), (self.y, 0)]):
            copy = remote(self.half(self.src, h), self.half(mine, h), self.sems, at, to)
            copy.start()
            self.out.append(copy)
        held = pl.ds(0, self.wide)
        self.keep = pltpu.make_async_copy(self.src.at[held], mine.at[held], self.own_sem)
        self.keep.start()
        self.tails = []
        self.tail(self.src, self.rep, 0)

    def tail(self, shard, origin, at):
        more = self.slots - self.wide
        if more == 0:
            return
        copy = remote(
            shard.at[pl.ds(self.wide - more, more)],
            self.dst.at[origin, pl.ds(self.wide, more)],
            self.tail_sems, at, self.sibling,
        )
        copy.start()
        self.tails.append(copy)

    def forward(self):
        from_x, from_y = self.dst.at[self.x_rep], self.dst.at[self.y_rep]
        self.out[0].wait_recv()
        copy = remote(self.half(from_x, 0), self.half(from_x, 0), self.sems, 4, self.y)
        copy.start()
        self.out.append(copy)
        self.out[1].wait_recv()
        copy = remote(self.half(from_y, 1), self.half(from_y, 1), self.sems, 5, self.x)
        copy.start()
        self.out.append(copy)

    def finish(self):
        self.out[2].wait_recv()
        self.tail(self.dst.at[self.x_rep], self.x_rep, 1)
        self.out[3].wait_recv()
        self.tail(self.dst.at[self.y_rep], self.y_rep, 2)
        self.out[4].wait_recv()
        self.out[5].wait_recv()
        self.tail(self.dst.at[self.d_rep], self.d_rep, 3)
        self.keep.wait()
        for copy in self.out:
            copy.wait_send()
        for copy in self.tails:
            copy.wait()


class Exchange:
    def __init__(self, chips, depth, share, src, dst, own_sem, sems, pass_sems):
        rep, work = lax.axis_index("replica"), lax.axis_index("fsdp")
        self.chips, self.depth, self.share = chips, depth, share
        self.src, self.dst = src, dst
        self.own_sem, self.sems, self.pass_sems = own_sem, sems, pass_sems
        self.chip, self.core = work // 2, work % 2
        self.rep = rep
        self.sibling = (rep, self.chip * 2 + 1 - self.core)

    def peer(self, d):
        return lax.rem(self.chip + d, self.chips)

    def device(self, d):
        return (self.rep, self.peer(d) * 2 + self.core)

    def devices(self):
        peers = [self.device(d) for d in range(1, self.chips)]
        return peers + ([self.sibling] if self.share else [])

    def landing(self, p):
        part = pl.ds(0, self.depth)
        return self.dst.at[self.core, p, part] if self.share else self.dst.at[p, part]

    def start(self):
        here = self.landing(self.chip)
        self.out = []
        for d in range(1, self.chips):
            copy = remote(self.src.at[self.peer(d)], here, self.sems, d, self.device(d))
            copy.start()
            self.out.append(copy)
        self.keep = pltpu.make_async_copy(self.src.at[self.chip], here, self.own_sem)
        self.keep.start()
        self.passes = []
        if self.share:
            copy = remote(self.src.at[self.chip], here, self.pass_sems, 0, self.sibling)
            copy.start()
            self.passes.append(copy)

    def forward(self):
        for d in range(1, self.chips):
            self.out[d - 1].wait_recv()
            if self.share:
                came = self.landing(lax.rem(self.chip + self.chips - d, self.chips))
                copy = remote(came, came, self.pass_sems, d, self.sibling)
                copy.start()
                self.passes.append(copy)

    def finish(self):
        self.keep.wait()
        for copy in self.out:
            copy.wait_send()
        for copy in self.passes:
            copy.wait()


def pair_of(n):
    return [pltpu.SemaphoreType.DMA((n,)), pltpu.SemaphoreType.DMA((n,))]


def remote_call(body, shapes, scratch, collective_id, name, size):
    anywhere = pl.BlockSpec(memory_space=pl.ANY)

    def call(*args):
        return pl.pallas_call(
            body,
            out_shape=[jax.ShapeDtypeStruct(shape, jnp.bfloat16) for shape in shapes],
            in_specs=[anywhere] * len(args),
            out_specs=[anywhere] * len(shapes),
            scratch_shapes=scratch,
            compiler_params=pltpu.CompilerParams(
                collective_id=collective_id, has_side_effects=True, vmem_limit_bytes=VMEM
            ),
            cost_estimate=pl.CostEstimate(flops=0, bytes_accessed=size, transcendentals=0),
            name=name,
        )(*args)

    return call


def bring_in(outgoing, root, wide, most, collective_id):
    chips, depth, rows, quarter = outgoing.shape

    def body(src, root_ref, dst, all_ref, own, ex_s, ex_r, pass_s, pass_r, ga_s, ga_r, ta_s, ta_r):
        ex = Exchange(chips, depth, True, src, dst, own.at[0], (ex_s, ex_r), (pass_s, pass_r))
        ga = Gather(wide, root_ref, all_ref, own.at[1], (ga_s, ga_r), (ta_s, ta_r))
        others = ex.devices()
        greet(others + ga.devices()[:2])
        ex.start()
        ga.start()
        ga.forward()
        ex.forward()
        ga.finish()
        ex.finish()

    shapes = [(2, chips, most, rows, quarter), (REPLICAS,) + root.shape]
    scratch = [pltpu.SemaphoreType.DMA((2,))]
    scratch += pair_of(chips) + pair_of(chips) + pair_of(6) + pair_of(4)
    size = 64 * outgoing.size
    return remote_call(body, shapes, scratch, collective_id, "bring_in", size)(outgoing, root)


def gather_slots(shard, wide, collective_id):
    def body(src, dst, own, ga_s, ga_r, ta_s, ta_r):
        ga = Gather(wide, src, dst, own, (ga_s, ga_r), (ta_s, ta_r))
        greet(ga.devices())
        ga.start()
        ga.forward()
        ga.finish()

    scratch = [pltpu.SemaphoreType.DMA] + pair_of(6) + pair_of(4)
    size = 16 * shard.size
    shapes = [(REPLICAS,) + shard.shape]
    return remote_call(body, shapes, scratch, collective_id, "gather_slots", size)(shard)[0]


def send_home(outgoing, most, collective_id):
    chips, depth, rows, quarter = outgoing.shape

    def body(src, dst, own, ex_s, ex_r):
        ex = Exchange(chips, depth, False, src, dst, own, (ex_s, ex_r), None)
        greet(ex.devices())
        ex.start()
        ex.forward()
        ex.finish()

    scratch = [pltpu.SemaphoreType.DMA] + pair_of(chips)
    size = 64 * outgoing.size
    shapes = [(chips, most, rows, quarter)]
    return remote_call(body, shapes, scratch, collective_id, "send_home", size)(outgoing)[0]


def wire_body(own_at, sib_at, use_sib, own_ref, sib_ref, out_ref):
    t = pl.program_id(0)

    @pl.when(use_sib[t] > 0)
    def _():
        out_ref[...] = sib_ref[...]

    @pl.when(use_sib[t] == 0)
    def _():
        out_ref[...] = own_ref[...]


def wire_slots(own, sib, own_at, sib_at, use_sib):
    block = (1,) + own.shape[1:]
    return pl.pallas_call(
        wire_body,
        grid_spec=pltpu.PrefetchScalarGridSpec(
            num_scalar_prefetch=3,
            grid=(own.shape[0],),
            in_specs=[
                pl.BlockSpec(block, lambda t, own_at, sib_at, use_sib: (own_at[t], 0, 0)),
                pl.BlockSpec(block, lambda t, own_at, sib_at, use_sib: (sib_at[t], 0, 0)),
            ],
            out_specs=pl.BlockSpec(block, lambda t, *_: (t, 0, 0)),
        ),
        out_shape=jax.ShapeDtypeStruct(own.shape, own.dtype),
        compiler_params=pltpu.CompilerParams(vmem_limit_bytes=VMEM),
        name="wire_slots",
    )(own_at, sib_at, use_sib, own, sib)


def step_body(
    ints, lscale, rscale, width, g_ref, l_ref, r_ref, ls_ref, rs_ref,
    ln_ref, rn_ref, pre_ref, sq_ref,
):
    s = pl.program_id(0)
    me, count = ints[0], ints[1]
    n, _, size, quarter = g_ref.shape
    nt = (((1,), (1,)), ((), ()))
    tn = (((0,), (0,)), ((), ()))
    keep = 1.0 - SHRINKAGE
    rows = lax.broadcasted_iota(jnp.int32, (quarter, quarter), 0)
    cols = lax.broadcasted_iota(jnp.int32, (quarter, quarter), 1)
    unit = rows == cols
    first = pl.multiple_of(me * quarter, quarter)

    @pl.when(s < count)
    def _():
        gram = None
        for r in range(n):
            part = lax.dot_general(
                g_ref[r, 0, pl.ds(first, quarter), :], g_ref[r, 0], nt,
                preferred_element_type=jnp.float32,
            )
            gram = part if gram is None else gram + part
        ln_ref[0] = (keep * DECAY) * ls_ref[0] + (keep * (1.0 - DECAY)) * gram
        mine = g_ref[me, 0]
        for r in range(n):
            at = pl.ds(r * quarter, quarter)
            part = lax.dot_general(mine, g_ref[r, 0], tn, preferred_element_type=jnp.float32)
            rn_ref[0, :, at] = (keep * DECAY) * rs_ref[0, :, at] + (keep * (1.0 - DECAY)) * part
        inner = None
        for r in range(n):
            part = jnp.dot(
                g_ref[r, 0], r_ref[0, pl.ds(r * quarter, quarter), :],
                preferred_element_type=jnp.float32,
            )
            inner = part if inner is None else inner + part
        inner = inner.astype(jnp.bfloat16)
        out = None
        for r in range(n):
            part = jnp.dot(
                l_ref[r, 0], inner[r * quarter : (r + 1) * quarter],
                preferred_element_type=jnp.float32,
            )
            out = part if out is None else out + part
        column = lax.broadcasted_iota(jnp.int32, out.shape, 1) + first
        out = jnp.where(column < width[s], out, 0.0)
        sq_ref[0] = jnp.sum(out * out, axis=0, keepdims=True)
        pre_ref[0] = out.astype(jnp.bfloat16)

    @pl.when(s >= count)
    def _():
        ln_ref[0] = (keep * DECAY) * ls_ref[0]
        rn_ref[0] = (keep * DECAY) * rs_ref[0]
        sq_ref[...] = jnp.zeros_like(sq_ref)
        pre_ref[...] = jnp.zeros_like(pre_ref)

    here = pl.ds(first, quarter)
    ln_ref[0, :, here] += jnp.where(unit, lscale[s], 0.0)
    rn_ref[0, :, here] += jnp.where(unit & (rows + first < width[s]), rscale[s], 0.0)


def step_slots(ints, lscale, rscale, width, g_all, l_all, right_root, left_stat, right_stat):
    n, slots, size, quarter = g_all.shape

    def used(s, ints):
        return jnp.minimum(s, jnp.maximum(ints[1] - 1, 0))

    def held(s, ints):
        at = used(s, ints)
        return jnp.where(at < ints[2], at, at + slots - ints[1])

    gathered = pl.BlockSpec((n, 1, size, quarter), lambda s, ints, *_: (0, held(s, ints), 0, 0))
    tall = pl.BlockSpec((1, size, quarter), lambda s, ints, *_: (used(s, ints), 0, 0))
    stat = pl.BlockSpec((1, quarter, size), lambda s, *_: (s, 0, 0))
    return pl.pallas_call(
        step_body,
        grid_spec=pltpu.PrefetchScalarGridSpec(
            num_scalar_prefetch=4,
            grid=(slots,),
            in_specs=[gathered, gathered, tall, stat, stat],
            out_specs=[
                stat,
                stat,
                pl.BlockSpec((1, size, quarter), lambda s, *_: (s, 0, 0)),
                pl.BlockSpec((1, 1, quarter), lambda s, *_: (s, 0, 0)),
            ],
        ),
        out_shape=[
            jax.ShapeDtypeStruct(left_stat.shape, jnp.float32),
            jax.ShapeDtypeStruct(right_stat.shape, jnp.float32),
            jax.ShapeDtypeStruct((slots, size, quarter), jnp.bfloat16),
            jax.ShapeDtypeStruct((slots, 1, quarter), jnp.float32),
        ],
        compiler_params=pltpu.CompilerParams(vmem_limit_bytes=VMEM),
        name="step_slots",
    )(ints, lscale, rscale, width, g_all, l_all, right_root, left_stat, right_stat)


def load_body(slot, own, core, own_ref, sib_ref, out_ref):
    p, k = pl.program_id(0), pl.program_id(1)

    @pl.when(own[p, k] > 0)
    def _():
        out_ref[0, 0] = own_ref[0, 0, 0]

    @pl.when(own[p, k] == 0)
    def _():
        out_ref[0, 0] = sib_ref[0, 0]


def load_outgoing(mine, sibling, slot, own, core, chips, depth):
    _, hosts, _, rows, quarter = mine.shape
    return pl.pallas_call(
        load_body,
        grid_spec=pltpu.PrefetchScalarGridSpec(
            num_scalar_prefetch=3,
            grid=(chips, depth),
            in_specs=[
                pl.BlockSpec(
                    (1, 1, 1, rows, quarter),
                    lambda p, k, slot, own, core: (slot[p, k], p % hosts, core[0], 0, 0),
                ),
                pl.BlockSpec(
                    (1, 1, rows, quarter),
                    lambda p, k, slot, own, core: (slot[p, k], p % hosts, 0, 0),
                ),
            ],
            out_specs=pl.BlockSpec((1, 1, rows, quarter), lambda p, k, *_: (p, k, 0, 0)),
        ),
        out_shape=jax.ShapeDtypeStruct((chips, depth, rows, quarter), jnp.bfloat16),
        compiler_params=pltpu.CompilerParams(vmem_limit_bytes=VMEM),
        name="load_outgoing",
    )(slot, own, core, mine, sibling)


def assemble_body(chip, rank, scale, in_ref, out_ref):
    j = pl.program_id(0)
    out_ref[0] = (in_ref[0, 0].astype(jnp.float32) * scale[j]).astype(jnp.bfloat16)


def assemble(got, chip, rank, scale):
    _, _, rows, quarter = got.shape
    return pl.pallas_call(
        assemble_body,
        grid_spec=pltpu.PrefetchScalarGridSpec(
            num_scalar_prefetch=3,
            grid=(chip.shape[0],),
            in_specs=[
                pl.BlockSpec(
                    (1, 1, rows, quarter), lambda j, chip, rank, scale: (chip[j], rank[j], 0, 0)
                )
            ],
            out_specs=pl.BlockSpec((1, rows, quarter), lambda j, *_: (j, 0, 0)),
        ),
        out_shape=jax.ShapeDtypeStruct((chip.shape[0], rows, quarter), jnp.bfloat16),
        compiler_params=pltpu.CompilerParams(vmem_limit_bytes=VMEM),
        name="assemble",
    )(chip, rank, scale, got)


def on_device(grad_parts, col_widths, assignment, left_stat, right_stat, left_root, right_root):
    workers = lax.axis_size("fsdp")
    me_rep = lax.axis_index("replica")
    me_work = lax.axis_index("fsdp")
    slots, quarter, block_size = left_stat.shape
    rows_dev, ncols = grad_parts.shape[1:3]
    per_row = block_size // rows_dev
    chips = workers // 2
    hosts = per_row // 2
    chip, core = me_work // 2, me_work % 2
    most = min(ncols, 2 * slots)
    cases = [k for k in DEPTHS if k < most] + [most]
    widths = [k for k in WIDTHS if slots <= 2 * k and k < slots] + [slots]
    slot_rank, filled, block_ids = slot_tables(assignment, workers, slots)
    blocks = jnp.arange(assignment.shape[0], dtype=jnp.int32)
    of_row = blocks // ncols
    of_chip = assignment // 2
    pair = of_row * chips + of_chip
    pair_rank = jnp.sum(
        ((pair[:, None] == pair[None, :]) & (blocks[None, :] < blocks[:, None])).astype(jnp.int32),
        axis=1,
    )
    depth = jnp.max(pair_rank) + 1
    case = jnp.sum((depth > jnp.array(cases, jnp.int32)).astype(jnp.int32))
    chip_load = jnp.sum(
        (of_chip[None, :] == jnp.arange(chips, dtype=jnp.int32)[:, None]).astype(jnp.int32), axis=1
    )
    load = jnp.max(chip_load)
    width_case = jnp.sum((load > 2 * jnp.array(widths, jnp.int32)).astype(jnp.int32))
    wide = jnp.array(widths, jnp.int32)[width_case]
    owner_first = me_work // per_row * ncols
    row_chip = lax.dynamic_slice_in_dim(of_chip, owner_first, ncols)
    row_rank = lax.dynamic_slice_in_dim(pair_rank, owner_first, ncols)
    all_chips = jnp.arange(chips, dtype=jnp.int32)
    ranks = jnp.arange(most, dtype=jnp.int32)
    leaves = (row_chip == all_chips[:, None, None]) & (row_rank == ranks[None, :, None])
    send_col = jnp.sum(jnp.where(leaves, jnp.arange(ncols, dtype=jnp.int32), 0), axis=2)
    returns = (
        (of_chip == chip)
        & (of_row == (all_chips // hosts)[:, None, None])
        & (pair_rank == ranks[None, :, None])
    )
    back_slot = jnp.sum(jnp.where(returns, slot_rank, 0), axis=2)
    back_own = jnp.sum((returns & (assignment == me_work)).astype(jnp.int32), axis=2)

    def choose(index, makers, *args):
        if len(makers) == 1:
            return makers[0](*args)
        return lax.switch(index, makers, *args)

    sib_work = chip * 2 + 1 - core
    sib_count = jnp.sum((assignment == sib_work).astype(jnp.int32))
    kept = wide - jnp.maximum(sib_count - wide, 0)
    wires = jnp.arange(slots, dtype=jnp.int32)
    lent = (wires >= kept) & (wires < wide)
    lent_slot = jnp.clip(wide + wires - kept, 0, slots - 1)
    wire_slot = jnp.where(lent, sib_work * slots + lent_slot, me_work * slots + wires)
    wire_block = jnp.take(block_ids, wire_slot)
    wire_live = (jnp.take(filled, wire_slot) & (wires < wide)).astype(jnp.int32)
    swap = [(w, w + 1 - 2 * (w % 2)) for w in range(workers)]
    root = left_root
    if len(widths) > 1:
        low = widths[0]
        sib_root = lax.ppermute(left_root[low:], "fsdp", swap)
        root = wire_slots(
            left_root,
            sib_root,
            jnp.where(lent, 0, wires),
            jnp.where(lent, lent_slot - low, 0),
            lent.astype(jnp.int32),
        )

    summed = lax.psum_scatter(grad_parts[0], "replica", scatter_dimension=2, tiled=True)

    my_blocks = lax.dynamic_slice_in_dim(block_ids, me_work * slots, slots)
    my_filled = lax.dynamic_slice_in_dim(filled, me_work * slots, slots)
    my_count = jnp.sum(my_filled.astype(jnp.int32))
    my_row = my_blocks // ncols
    my_col = my_blocks % ncols
    looked_up = jnp.sum(
        jnp.where(
            my_col[:, None] == jnp.arange(ncols, dtype=jnp.int32)[None, :], col_widths[None, :], 0
        ),
        axis=1,
    )
    my_width = jnp.where(my_filled, looked_up, block_size)

    first = me_rep * quarter
    global_rows = first + jnp.arange(quarter, dtype=jnp.int32)
    unit = jnp.eye(quarter, dtype=jnp.float32)
    within = (global_rows[None, :] < my_width[:, None]).astype(jnp.float32)
    left_diag = jnp.sum(lax.dynamic_slice_in_dim(left_stat, first, quarter, 2) * unit, axis=2)
    right_diag = jnp.sum(lax.dynamic_slice_in_dim(right_stat, first, quarter, 2) * unit, axis=2)
    left_part = jnp.sum(left_diag, axis=1)
    right_part = jnp.sum(right_diag * within, axis=1)

    col_mask = global_rows[None, :] < col_widths[:, None]
    masked = jnp.where(col_mask[None], summed, jnp.zeros((), jnp.bfloat16))

    def send_in(n, by_block, col, root):
        k, w = cases[n // len(widths)], widths[n % len(widths)]
        return bring_in(fill_outgoing(by_block, col, chips, k), root, w, most, n)

    pairs = len(cases) * len(widths)
    got, left_wide = choose(
        case * len(widths) + width_case,
        [functools.partial(send_in, n) for n in range(pairs)],
        jnp.transpose(masked, (1, 0, 2)),
        send_col,
        root,
    )
    my_live = my_filled.astype(jnp.int32)
    g_cols, g_sq = pick_blocks(
        got,
        (wire_block // ncols, jnp.take(pair_rank, wire_block), wire_live),
        (my_row, jnp.take(pair_rank, my_blocks), my_live),
        block_size,
    )

    def spread_slots(n, shard):
        return gather_slots(shard, widths[n], pairs + n)

    g_all = choose(
        width_case, [functools.partial(spread_slots, n) for n in range(len(widths))], g_cols
    )
    left_trace, right_trace, grad_square = lax.psum(
        (left_part, right_part, jnp.sum(g_sq, axis=(1, 2))), "replica"
    )
    left_scale = SHRINKAGE * (DECAY * left_trace + (1.0 - DECAY) * grad_square) / block_size
    right_scale = (
        SHRINKAGE
        * (DECAY * right_trace + (1.0 - DECAY) * grad_square)
        / my_width.astype(jnp.float32)
    )
    ints = jnp.stack([me_rep.astype(jnp.int32), my_count, wide])
    left_new, right_new, precond, p_sq = step_slots(
        ints, left_scale, right_scale, my_width, g_all, left_wide, right_root, left_stat, right_stat
    )
    split = precond.reshape(slots, hosts, 2, rows_dev, quarter)
    crossing = lax.dynamic_index_in_dim(split, 1 - core, 2, keepdims=False)
    sibling = lax.ppermute(crossing, "fsdp", swap)

    def send_back(n, mine, other, slot, own, core):
        outgoing = load_outgoing(mine, other, slot, own, core, chips, cases[n])
        return send_home(outgoing, most, pairs + len(widths) + n)

    back = choose(
        case,
        [functools.partial(send_back, n) for n in range(len(cases))],
        split,
        sibling,
        back_slot,
        back_own,
        core[None],
    )
    squares = jnp.stack([grad_square / REPLICAS, jnp.sum(p_sq, axis=(1, 2))])
    placed = lax.dynamic_update_slice(
        jnp.zeros((2, workers * slots), jnp.float32), squares, (0, me_work * slots)
    )
    placed = lax.psum(placed, ("replica", "fsdp"))
    every_scale = jnp.sqrt(placed[0] / (placed[1] + EPSILON))
    owner_worker = lax.dynamic_slice_in_dim(assignment, owner_first, ncols)
    owner_slot = lax.dynamic_slice_in_dim(slot_rank, owner_first, ncols)
    my_scale = jnp.take(every_scale, owner_worker * slots + owner_slot)
    arrived = assemble(back, row_chip, row_rank, my_scale)
    update = jnp.transpose(arrived, (1, 0, 2))
    return (update, left_new, right_new)


def solution(mesh):
    in_specs = (
        P("replica", "fsdp", None, None),
        P(),
        P(),
        P("fsdp", "replica", None),
        P("fsdp", "replica", None),
        P("fsdp", None, "replica"),
        P("fsdp", None, "replica"),
    )
    out_specs = (P("fsdp", None, "replica"), P("fsdp", "replica", None), P("fsdp", "replica", None))
    return jax.shard_map(
        on_device, mesh=mesh, in_specs=in_specs, out_specs=out_specs, check_vma=False
    )
```
